32 devices in a mesh: mem: 16 (over z, x, core), dec: 2 (over y).
Axes of the slice: x: 2, y: 2, z: 4, core: 2. Of those that a mesh axis runs over, the one named last changes fastest.
Arguments:
- question_states: bfloat16 [16, 8, 4096], P('mem', None, 'dec'), may hold values from -6 to 6
- passage_cache: bfloat16 [64, 64, 4096], P('mem', None, 'dec'), may hold values from -6 to 6
- norm_gain: float32 [4096], replicated, may hold values from 0.1 to 1.9
- enc_wq: bfloat16 [4096, 2048], P('mem', 'dec'), may hold values from -0.09375 to 0.09375
- enc_wk: bfloat16 [4096, 2048], P('mem', 'dec'), may hold values from -0.09375 to 0.09375
- enc_wv: bfloat16 [4096, 2048], P('mem', 'dec'), may hold values from -0.09375 to 0.09375
- enc_wo: bfloat16 [2048, 4096], P('dec', 'mem'), may hold values from -0.125 to 0.125
- dec_wk: bfloat16 [4096, 2048], P('dec'), may hold values from -0.09375 to 0.09375
- dec_wv: bfloat16 [4096, 2048], P('dec'), may hold values from -0.09375 to 0.09375
- dec_queries: bfloat16 [16, 8, 2048], P('mem', None, 'dec'), may hold values from -6 to 6
- passage_ids: int32 [16, 2], replicated, may hold values from 0 to 63, as said below
- location: int32 [64], replicated, may hold values from 0 to 63, as said below
- question_lengths: int32 [16], replicated, may hold values from 1 to 8
Outputs:
- decoder_context: bfloat16 [16, 8, 2048], P('mem', None, 'dec')
The draws below stay inside these ranges and needn't reach their ends.
Inputs may be any that keep to these rules, and one draw needn't show every extreme that they name: `passage_ids`: the requests whose passage lies in cache rows s * 4 to (s + 1) * 4 - 1 number at most 3 for every s, and exactly 3 for some s; a question's passages need not differ. A permutation: passage p's states are row location[p] of passage_cache.
All inputs are finite; a program needn't handle non-finite values.
Results may differ from the reference program's by a relative error of at most 0.04.
Values may be sent and summed in bfloat16 or wider, within the bound.
No kernel may reach another device: no remote copies, remote signals or barrier semaphores. Data moves between devices by JAX's collectives and lax.ppermute only.
A program may use at most 128 MiB of HBM per device.

```python
import jax
import jax.numpy as jnp
from jax import lax

D = 4096
HEADS = 32
HEAD_DIM = 64
P_SIZE = 64
QL = 8
KPASS = 2
ANS = 8
NP_DEV = 4
HD = 2048
Q = 16
NPASS = 64
N_DEC = 2


def shared_layout(key):
    location = jax.random.permutation(jax.random.fold_in(key, 11), NPASS).astype(jnp.int32)
    count_table = jnp.array([[3, 3, 2, 0], [3, 2, 2, 1], [3, 3, 1, 1], [2, 2, 2, 2], [1, 2, 2, 3], [0, 2, 3, 3]], jnp.int32)
    pattern_pick = jax.random.randint(jax.random.fold_in(key, 12), (Q // 4,), 0, 6)
    pattern_pick = pattern_pick.at[0].set(0)
    ranked_counts = count_table[pattern_pick].reshape(-1)
    owner_order = jax.random.permutation(jax.random.fold_in(key, 13), Q)
    counts = jnp.zeros((Q,), jnp.int32).at[owner_order].set(ranked_counts)
    request_total = Q * KPASS
    bounds = jnp.cumsum(counts)
    request_owner = jnp.sum((bounds[None, :] <= jnp.arange(request_total)[:, None]).astype(jnp.int32), axis=1)
    shuffled = jax.random.permutation(jax.random.fold_in(key, 14), request_total)
    request_owner = request_owner[shuffled]
    slot_pick = jax.random.randint(jax.random.fold_in(key, 15), (request_total,), 0, NP_DEV)
    cache_row = request_owner * NP_DEV + slot_pick
    inverse = jnp.argsort(location)
    passage_ids = inverse[cache_row].reshape(Q, KPASS).astype(jnp.int32)
    return (location, passage_ids)


def draw_location(key, part):
    return shared_layout(key)[0]


def draw_passage_ids(key, part):
    return shared_layout(key)[1]


def touch_ends(values, own_key, least, top_value):
    longest = values.shape.index(max(values.shape))
    spots = []
    for shift in (0, 1):
        where = [jax.random.randint(jax.random.fold_in(own_key, axis), (), 0, length) for axis, length in enumerate(values.shape)]
        where[longest] = (where[longest] + shift) % values.shape[longest]
        spots.append(tuple(where))
    return values.at[spots[0]].set(least).at[spots[1]].set(top_value)


def levels(rng, dims, pieces, low, largest):
    gain, own = 1.0, jax.random.fold_in(rng, 6)
    for dim, shards_of in pieces:
        heights = jnp.exp(jax.random.uniform(jax.random.fold_in(own, dim), (shards_of,), jnp.float32, low / len(pieces), largest / len(pieces)))
        gain = gain * jnp.repeat(heights, dims[dim] // shards_of).reshape([-1 if axis == dim else 1 for axis in range(len(dims))])
    return gain


def normal_values(rng, shape, deviation, bound, shards=(), kind=jnp.bfloat16):
    values = deviation * jax.random.normal(rng, shape, jnp.float32)
    if shards:
        values = values * levels(rng, shape, shards, -0.22, 0.18)
    return jnp.clip(values, -bound, bound).astype(kind)


def setup_inputs(seed: int = 0) -> dict:
    arg_keys = jax.random.split(jax.random.key(seed), 14)
    return {
        "question_states": normal_values(arg_keys[0], (Q, QL, D), 1.0, 6.0, ((0, 16), (2, 2))),
        "passage_cache": normal_values(arg_keys[1], (NPASS, P_SIZE, D), 1.0, 6.0, ((0, 16), (2, 2))),
        "norm_gain": jnp.clip(1.0 + 0.18 * jax.random.normal(arg_keys[2], (D,), jnp.float32), 0.1, 1.9),
        "enc_wq": normal_values(arg_keys[3], (D, HD), D ** -0.5, 0.09375, ((0, 16), (1, 2))),
        "enc_wk": normal_values(arg_keys[4], (D, HD), D ** -0.5, 0.09375, ((0, 16), (1, 2))),
        "enc_wv": normal_values(arg_keys[5], (D, HD), D ** -0.5, 0.09375, ((0, 16), (1, 2))),
        "enc_wo": normal_values(arg_keys[6], (HD, D), HD ** -0.5, 0.125, ((0, 2), (1, 16))),
        "dec_wk": normal_values(arg_keys[7], (D, HD), D ** -0.5, 0.09375, ((0, 2),)),
        "dec_wv": normal_values(arg_keys[8], (D, HD), D ** -0.5, 0.09375, ((0, 2),)),
        "dec_queries": normal_values(arg_keys[9], (Q, ANS, HD), 1.0, 6.0, ((0, 16), (2, 2))),
        "passage_ids": draw_passage_ids(jax.random.fold_in(arg_keys[13], 71), 0),
        "location": draw_location(jax.random.fold_in(arg_keys[13], 71), 0),
        "question_lengths": touch_ends(jax.random.randint(arg_keys[12], (Q,), 1, QL + 1), jax.random.fold_in(arg_keys[12], 1), 1, QL).astype(jnp.int32),
    }


NORM_EPSILON = 1e-06

def rounded(value):
    return lax.optimization_barrier(value.astype(jnp.bfloat16))

def reference(question_states, passage_cache, norm_gain, enc_wq, enc_wk, enc_wv, enc_wo, dec_wk, dec_wv, dec_queries, passage_ids, location, question_lengths):
    hd_total = HEADS * HEAD_DIM
    pair_rows = QL + P_SIZE
    group_heads = hd_total // N_DEC
    group_width = D // N_DEC
    score_scale = HEAD_DIM ** (-0.5)
    positions = jnp.arange(pair_rows)

    def one_question(question_index):
        cache_rows = location[passage_ids[question_index]]
        passages = passage_cache[cache_rows]
        own_states = jnp.broadcast_to(question_states[question_index][None], (KPASS, QL, D))
        widened = jnp.concatenate([own_states, passages], axis=1).astype(jnp.float32)
        squares = lax.optimization_barrier(jnp.mean(widened * widened, axis=2, keepdims=True))
        normed = rounded(widened * lax.rsqrt(squares + NORM_EPSILON) * norm_gain).reshape(KPASS * pair_rows, D)
        shape_four = (KPASS, pair_rows, HEADS, HEAD_DIM)
        queries = rounded(jnp.dot(normed, enc_wq, preferred_element_type=jnp.float32)).astype(jnp.float32).reshape(shape_four)
        enc_keys = rounded(jnp.dot(normed, enc_wk, preferred_element_type=jnp.float32)).astype(jnp.float32).reshape(shape_four)
        enc_values = rounded(jnp.dot(normed, enc_wv, preferred_element_type=jnp.float32)).astype(jnp.float32).reshape(shape_four)
        live_keys = ((positions >= QL) | (positions < question_lengths[question_index])).astype(jnp.float32)
        scores = jnp.einsum('cihe,cjhe->chij', queries, enc_keys) * score_scale
        weights = jnp.exp(scores) * live_keys[None, None, None, :]
        probabilities = rounded(weights / lax.optimization_barrier(jnp.sum(weights, axis=3, keepdims=True))).astype(jnp.float32)
        context = rounded(jnp.einsum('chij,cjhe->cihe', probabilities, enc_values)).reshape(KPASS * pair_rows, hd_total)
        attended = jnp.zeros((KPASS * pair_rows, D), jnp.float32)
        for group_index in range(N_DEC):
            low = group_index * group_heads
            group_part = jnp.dot(context[:, low:low + group_heads], enc_wo[low:low + group_heads], preferred_element_type=jnp.float32)
            attended = attended + rounded(group_part).astype(jnp.float32)
        encoded = rounded(widened.reshape(KPASS * pair_rows, D) + attended)
        key_sum = jnp.zeros((KPASS * pair_rows, hd_total), jnp.float32)
        value_sum = jnp.zeros((KPASS * pair_rows, hd_total), jnp.float32)
        for group_index in range(N_DEC):
            low = group_index * group_width
            block = encoded[:, low:low + group_width]
            key_sum = key_sum + rounded(jnp.dot(block, dec_wk[low:low + group_width], preferred_element_type=jnp.float32)).astype(jnp.float32)
            value_sum = value_sum + rounded(jnp.dot(block, dec_wv[low:low + group_width], preferred_element_type=jnp.float32)).astype(jnp.float32)
        dec_keys = rounded(key_sum).astype(jnp.float32).reshape(shape_four)
        dec_values = rounded(value_sum).astype(jnp.float32).reshape(shape_four)
        asked = dec_queries[question_index].astype(jnp.float32).reshape(ANS, HEADS, HEAD_DIM)
        cross_scores = jnp.einsum('ahe,cjhe->hacj', asked, dec_keys) * score_scale
        cross_weight = jnp.exp(cross_scores) * live_keys[None, None, None, :]
        numerators = jnp.einsum('hacj,cjhe->ahe', rounded(cross_weight).astype(jnp.float32), dec_values)
        denominators = jnp.transpose(lax.optimization_barrier(jnp.sum(cross_weight, axis=(2, 3))))
        return (numerators / denominators[:, :, None]).reshape(ANS, hd_total).astype(jnp.bfloat16)
    return lax.map(one_question, jnp.arange(Q).astype(jnp.int32))
```

```python
import jax
import jax.numpy as jnp
from jax import lax
from jax.experimental import pallas as pl
from jax.experimental.pallas import tpu as pltpu
from jax.sharding import PartitionSpec as P

HEAD_DIM = 64
CAP = 3


NORM_EPSILON = 1e-06


def split_mem(mem_count):
    line_count = 1 << (mem_count.bit_length() // 2)
    return line_count, mem_count // line_count


def bits_of(inner_count):
    return [1 << k for k in range(inner_count.bit_length() - 1)]


def swap_mem(value, mask, mem_count):
    return lax.ppermute(value, "mem", [(i, i ^ mask) for i in range(mem_count)])


def over_dec(value, dec_index, dec_count):
    parts = [value]
    for step in range(1, dec_count):
        parts.append(
            lax.ppermute(value, "dec", [(i, (i - step) % dec_count) for i in range(dec_count)])
        )
    twice = jnp.stack(parts + parts)
    ordered = lax.dynamic_slice_in_dim(twice, (dec_count - dec_index) % dec_count, dec_count, 0)
    return jnp.moveaxis(ordered, 0, -2).reshape(value.shape[:-1] + (dec_count * value.shape[-1],))


def over_dec_halves(value, upper, dec_index, dec_count):
    if dec_count == 2:
        other = lax.ppermute(value, "dec", [(0, 1), (1, 0)])
        same = upper == (dec_index == 1)
        return jnp.where(same, value, other), jnp.where(same, other, value)
    whole = over_dec(value, dec_index, dec_count)
    half = whole.shape[1] // 2
    low, high = whole[:, :half], whole[:, half:]
    return jnp.where(upper, high, low), jnp.where(upper, low, high)


def dec_sum(value, dec_count):
    total = value
    for step in range(1, dec_count):
        total = total + lax.ppermute(
            value, "dec", [(i, (i + step) % dec_count) for i in range(dec_count)]
        )
    return total


def shift_line(value, step, first, last, inner_count):
    pairs = [
        (at * inner_count + b, (at + step) * inner_count + b)
        for at in range(first, last)
        for b in range(inner_count)
    ]
    return lax.ppermute(value, "mem", pairs)


def gather_line(value, axis, line_index, line_count, inner_count):
    upward, downward = [value], [value]
    for step in range(1, line_count):
        upward.append(shift_line(upward[-1], 1, step - 1, line_count - 1, inner_count))
        downward.append(shift_line(downward[-1], -1, 1, line_count - step + 1, inner_count))
    ordered = jnp.concatenate(upward[:0:-1] + [value] + downward[1:], axis=axis)
    size = value.shape[axis]
    return lax.dynamic_slice_in_dim(
        ordered, (line_count - 1 - line_index) * size, line_count * size, axis
    )


def after(value, *earlier):
    return lax.optimization_barrier((value, *earlier))[0]


def along(sent, pairs, inner_count):
    return lax.ppermute(
        sent,
        "mem",
        [(a * inner_count + b, c * inner_count + b) for a, c in pairs for b in range(inner_count)],
    )


def beside(value, inner_count):
    return along(value, [(0, 1), (1, 0), (2, 3), (3, 2)], inner_count)


def far_half(near, line_index, inner_count):
    across = along(near, [(1, 2), (2, 1)], inner_count)
    outward = along(across, [(1, 0), (2, 3)], inner_count)
    middle = (line_index == 1) | (line_index == 2)
    return jnp.where(middle, across, outward)


def attention_kernel(heads, lives_ref, query_ref, key_ref, value_ref, out_ref):
    slots, rows, _ = query_ref.shape
    lanes = 2 * HEAD_DIM
    lane = lax.broadcasted_iota(jnp.int32, (rows, lanes), 1)
    key_at = lax.broadcasted_iota(jnp.int32, (rows, rows), 1)
    first = lane < HEAD_DIM
    for slot in range(slots):
        live = (key_at < lives_ref[0, slot]) | (key_at >= lives_ref[1, slot])
        for pair in range(heads // 2):
            span = slice(pair * lanes, (pair + 1) * lanes)
            query = query_ref[slot, :, span] * HEAD_DIM ** (-0.5)
            key = key_ref[slot, :, span].astype(jnp.bfloat16)
            value = value_ref[slot, :, span].astype(jnp.bfloat16)
            outs = []
            for chosen in (first, ~first):
                scores = lax.dot_general(
                    jnp.where(chosen, query, 0.0).astype(jnp.bfloat16),
                    key,
                    (((1,), (1,)), ((), ())),
                    preferred_element_type=jnp.float32,
                )
                weights = jnp.where(live, jnp.exp(scores), 0.0)
                total = jnp.sum(weights, axis=1, keepdims=True)
                probabilities = (weights / total).astype(jnp.bfloat16)
                outs.append(jnp.dot(probabilities, value, preferred_element_type=jnp.float32))
            out_ref[slot, :, span] = jnp.where(first, outs[0], outs[1])


def attend(lives, queries, keys, values):
    heads = queries.shape[2] // HEAD_DIM
    return pl.pallas_call(
        lambda *refs: attention_kernel(heads, *refs),
        out_shape=jax.ShapeDtypeStruct(queries.shape, jnp.float32),
        in_specs=[pl.BlockSpec(memory_space=pltpu.SMEM)]
        + [pl.BlockSpec(memory_space=pltpu.VMEM)] * 3,
        out_specs=pl.BlockSpec(memory_space=pltpu.VMEM),
        compiler_params=pltpu.CompilerParams(vmem_limit_bytes=24 * 1024 * 1024),
        cost_estimate=pl.CostEstimate(
            flops=4 * queries.shape[0] * queries.shape[1] ** 2 * queries.shape[2],
            bytes_accessed=16 * queries.size,
            transcendentals=queries.shape[0] * queries.shape[1] ** 2 * heads,
        ),
    )(lives, queries, keys, values)


def body(
    question_states,
    passage_cache,
    norm_gain,
    enc_wq,
    enc_wk,
    enc_wv,
    enc_wo,
    dec_wk,
    dec_wv,
    dec_queries,
    passage_ids,
    location,
    question_lengths,
):
    mem_count = lax.axis_size("mem")
    mem_index = lax.axis_index("mem")
    dec_count = lax.axis_size("dec")
    dec_index = lax.axis_index("dec")
    line_count, inner_count = split_mem(mem_count)
    line_index, inner_index = mem_index // inner_count, mem_index % inner_count
    pass_count = passage_ids.shape[1]
    request_total = mem_count * pass_count
    stored_count = passage_cache.shape[0]
    question_rows = question_states.shape[1]
    pair_rows = question_rows + passage_cache.shape[1]
    row_total = CAP * pair_rows
    answer_rows = dec_queries.shape[1]
    local_features = question_states.shape[2]
    heads_width = dec_queries.shape[2]
    heads_here = heads_width // HEAD_DIM
    score_scale = HEAD_DIM ** (-0.5)
    model_width = local_features * dec_count

    cache_row = jnp.take(location, passage_ids.reshape(-1))
    owner_index = cache_row // stored_count
    cache_slot = cache_row % stored_count
    served = (owner_index == mem_index).astype(jnp.int32)
    served_rank = jnp.cumsum(served) - 1
    taken_mask = (served[None, :] == 1) & (served_rank[None, :] == jnp.arange(CAP)[:, None])
    filled = jnp.any(taken_mask, axis=1)
    request = jnp.sum(jnp.where(taken_mask, jnp.arange(request_total)[None, :], 0), axis=1)
    asking = request // pass_count
    local_slot = jnp.sum(jnp.where(taken_mask, cache_slot[None, :], 0), axis=1)

    relay = line_count == 4
    if relay:
        query_beside = beside(enc_wq, inner_count)
    sent = jnp.concatenate([question_states, dec_queries], axis=2)
    sent = jnp.concatenate(
        [sent] + [swap_mem(sent, mask, mem_count) for mask in range(1, inner_count)], axis=0
    )
    came = [
        swap_mem(sent, mask, mem_count) for mask in range(inner_count, mem_count, inner_count)
    ]
    if relay:
        both_weights = after(jnp.concatenate([enc_wk, enc_wv], axis=0), came[0])
        both_beside = beside(both_weights, inner_count)
    sent = jnp.concatenate([sent] + came, axis=0)
    asked = sent[asking ^ mem_index]
    asked_states = asked[:, :, :local_features]
    asked_queries = over_dec(asked[:, :, local_features:], dec_index, dec_count)

    asked_passages = passage_cache[local_slot]
    local_rows = jnp.concatenate([asked_states, asked_passages], axis=1).reshape(row_total, -1)
    wide_rows = local_rows.astype(jnp.float32)
    squares = jnp.sum(jnp.square(wide_rows), axis=1, keepdims=True)
    row_scale = lax.rsqrt(dec_sum(squares, dec_count) / model_width + NORM_EPSILON)
    local_gain = lax.dynamic_slice_in_dim(norm_gain, dec_index * local_features, local_features)
    gained = (wide_rows * local_gain).astype(jnp.bfloat16)

    block = model_width // mem_count
    here = line_count // dec_count
    by_inner = gained.reshape(row_total, here, inner_count, block)

    def features_for(mask):
        picked = lax.dynamic_index_in_dim(by_inner, inner_index ^ mask, 2, keepdims=False)
        return picked.reshape(row_total, here * block)

    masks = [0]
    for bit in reversed(bits_of(inner_count)):
        masks = masks + [mask + bit for mask in masks]
    plane_rows = jnp.concatenate(
        [features_for(0)] + [swap_mem(features_for(k), k, mem_count) for k in masks[1:]], axis=0
    )
    upper = line_index >= line_count // 2
    near_rows, far_rows = over_dec_halves(plane_rows, upper, dec_index, dec_count)

    def halves(weight, weight_beside):
        if not relay:
            whole = gather_line(weight, 0, line_index, line_count, inner_count)
            half = whole.shape[0] // 2
            low, high = whole[:half], whole[half:]
            return jnp.where(upper, high, low), jnp.where(upper, low, high)
        near = jnp.where(
            line_index % 2 == 1,
            jnp.concatenate([weight_beside, weight], axis=0),
            jnp.concatenate([weight, weight_beside], axis=0),
        )
        return near, far_half(near, line_index, inner_count)

    def project(weight, weight_beside):
        near_weight, far_weight = halves(weight, weight_beside)

        def rows_sum(low, high):
            return jnp.dot(
                near_rows[low:high], near_weight, preferred_element_type=jnp.float32
            ) + jnp.dot(far_rows[low:high], far_weight, preferred_element_type=jnp.float32)

        rows = near_rows.shape[0]
        total = None
        for bit in bits_of(inner_count):
            rows //= 2
            if total is None:
                given, kept = rows_sum(rows, 2 * rows), rows_sum(0, rows)
            else:
                given, kept = total[rows:], total[:rows]
            total = kept + swap_mem(given.astype(jnp.bfloat16), bit, mem_count).astype(
                jnp.float32
            )
        return (total * row_scale).reshape(CAP, pair_rows, -1)

    block_rows = enc_wk.shape[0]
    besides = (
        (query_beside, both_beside[:block_rows], both_beside[block_rows:]) if relay else [None] * 3
    )
    queries, enc_keys, enc_values = (
        project(weight, near) for weight, near in zip((enc_wq, enc_wk, enc_wv), besides)
    )
    lengths_here = question_lengths[asking]
    positions = jnp.arange(pair_rows)
    live_keys = (
        (positions[None, :] >= question_rows) | (positions[None, :] < lengths_here[:, None])
    ).astype(jnp.float32)
    lives = jnp.stack([lengths_here, jnp.full_like(lengths_here, question_rows)])
    context = (
        attend(lives, queries, enc_keys, enc_values)
        .reshape(row_total, heads_width)
        .astype(jnp.bfloat16)
    )
    out_weight = lax.all_gather(after(enc_wo, plane_rows), "mem", axis=1, tiled=True)

    def out_columns(first, size):
        return jnp.dot(
            context,
            lax.dynamic_slice_in_dim(out_weight, first, size, 1),
            preferred_element_type=jnp.float32,
        )

    chunk = local_features // 2
    received = []
    for part in range(2):
        came = 0.0
        for step in range(1, dec_count):
            goal = (dec_index + step) % dec_count
            given = out_columns(goal * local_features + part * chunk, chunk).astype(jnp.bfloat16)
            came = came + lax.ppermute(
                given, "dec", [(i, (i + step) % dec_count) for i in range(dec_count)]
            ).astype(jnp.float32)
        received.append(came)
    kept = wide_rows + out_columns(dec_index * local_features, local_features)
    encoded = (kept + jnp.concatenate(received, axis=1)).astype(jnp.bfloat16)

    head_total = asked_queries.shape[2] // HEAD_DIM
    own_head = (
        jnp.arange(head_total * HEAD_DIM)[None, :] // HEAD_DIM == jnp.arange(head_total)[:, None]
    )
    spread = jnp.where(own_head[None, :, None, :], asked_queries[:, None], 0)
    wide_queries = lax.dot_general(
        spread.reshape(-1, head_total * HEAD_DIM),
        dec_wk,
        (((1,), (1,)), ((), ())),
        preferred_element_type=jnp.float32,
    ).astype(jnp.bfloat16)
    slot_rows = encoded.reshape(CAP, pair_rows, local_features)
    cross_scores = dec_sum(
        jnp.einsum(
            "cmf,cjf->cmj",
            wide_queries.reshape(CAP, head_total * answer_rows, local_features),
            slot_rows,
            preferred_element_type=jnp.float32,
        ),
        dec_count,
    )
    keep_keys = live_keys * filled.astype(jnp.float32)[:, None]
    cross_weight = jnp.exp(cross_scores * score_scale) * keep_keys[:, None, :]
    dec_values = jnp.dot(encoded, dec_wv, preferred_element_type=jnp.float32).astype(jnp.bfloat16)
    products = jnp.einsum(
        "cmj,cjv->cmv",
        cross_weight.astype(jnp.bfloat16),
        dec_values.reshape(CAP, pair_rows, -1),
        preferred_element_type=jnp.float32,
    ).reshape(CAP, head_total, answer_rows, -1)
    sums = jnp.sum(jnp.where(own_head[None, :, None, :], products, 0.0), axis=1)
    blocks = sums.reshape(CAP, answer_rows, dec_count, heads_width)

    def block_of(index):
        return lax.dynamic_index_in_dim(blocks, index, 2, keepdims=False)

    numerators = block_of(dec_index)
    for step in range(1, dec_count):
        numerators = numerators + lax.ppermute(
            block_of((dec_index + step) % dec_count).astype(jnp.bfloat16),
            "dec",
            [(i, (i + step) % dec_count) for i in range(dec_count)],
        ).astype(jnp.float32)
    every_denominator = jnp.sum(cross_weight, axis=2).reshape(CAP, head_total, answer_rows)
    denominators = lax.dynamic_slice_in_dim(
        every_denominator, dec_index * heads_here, heads_here, 1
    )
    both = jnp.concatenate(
        [
            numerators.reshape(CAP, -1),
            jnp.transpose(denominators, (0, 2, 1)).reshape(CAP, -1),
        ],
        axis=1,
    )
    targets = (
        (asking[:, None] == jnp.arange(mem_count)[None, :]) & filled[:, None]
    ).astype(jnp.float32)
    back = sum(targets[c][:, None] * both[c][None, :] for c in range(CAP))
    got = lax.all_to_all(
        back.astype(jnp.bfloat16), "mem", split_axis=0, concat_axis=0, tiled=True
    ).astype(jnp.float32)
    got_sum = jnp.sum(got, axis=0)
    numerator_sum = got_sum[: answer_rows * heads_width]
    denominator_sum = got_sum[answer_rows * heads_width :]
    answer = (
        numerator_sum.reshape(answer_rows, heads_here, HEAD_DIM)
        / denominator_sum.reshape(answer_rows, heads_here)[:, :, None]
    )
    return answer.reshape(1, answer_rows, heads_width).astype(jnp.bfloat16)


def solution(mesh):
    in_specs = (
        P("mem", None, "dec"),
        P("mem", None, "dec"),
        P(),
        P("mem", "dec"),
        P("mem", "dec"),
        P("mem", "dec"),
        P("dec", "mem"),
        P("dec", None),
        P("dec", None),
        P("mem", None, "dec"),
        P(),
        P(),
        P(),
    )
    out_specs = P("mem", None, "dec")
    return jax.shard_map(body, mesh=mesh, in_specs=in_specs, out_specs=out_specs, check_vma=False)
```

```python
import jax
import jax.numpy as jnp
from jax import lax
from jax.experimental import pallas as pl
from jax.experimental.pallas import tpu as pltpu
from jax.sharding import PartitionSpec as P

HEAD_DIM = 64
CAP = 3


NORM_EPSILON = 1e-06


def split_mem(mem_count):
    line_count = 1 << (mem_count.bit_length() // 2)
    return line_count, mem_count // line_count


def bits_of(inner_count):
    return [1 << k for k in range(inner_count.bit_length() - 1)]


def swap_mem(value, mask, mem_count):
    return lax.ppermute(value, "mem", [(i, i ^ mask) for i in range(mem_count)])


def over_dec(value, dec_index, dec_count):
    parts = [value]
    for step in range(1, dec_count):
        parts.append(
            lax.ppermute(value, "dec", [(i, (i - step) % dec_count) for i in range(dec_count)])
        )
    twice = jnp.stack(parts + parts)
    ordered = lax.dynamic_slice_in_dim(twice, (dec_count - dec_index) % dec_count, dec_count, 0)
    return jnp.moveaxis(ordered, 0, -2).reshape(value.shape[:-1] + (dec_count * value.shape[-1],))


def over_dec_halves(value, upper, dec_index, dec_count):
    if dec_count == 2:
        other = lax.ppermute(value, "dec", [(0, 1), (1, 0)])
        same = upper == (dec_index == 1)
        return jnp.where(same, value, other), jnp.where(same, other, value)
    whole = over_dec(value, dec_index, dec_count)
    half = whole.shape[1] // 2
    low, high = whole[:, :half], whole[:, half:]
    return jnp.where(upper, high, low), jnp.where(upper, low, high)


def dec_sum(value, dec_count):
    total = value
    for step in range(1, dec_count):
        total = total + lax.ppermute(
            value, "dec", [(i, (i + step) % dec_count) for i in range(dec_count)]
        )
    return total


def shift_line(value, step, first, last, inner_count):
    pairs = [
        (at * inner_count + b, (at + step) * inner_count + b)
        for at in range(first, last)
        for b in range(inner_count)
    ]
    return lax.ppermute(value, "mem", pairs)


def gather_line(value, axis, line_index, line_count, inner_count):
    upward, downward = [value], [value]
    for step in range(1, line_count):
        upward.append(shift_line(upward[-1], 1, step - 1, line_count - 1, inner_count))
        downward.append(shift_line(downward[-1], -1, 1, line_count - step + 1, inner_count))
    ordered = jnp.concatenate(upward[:0:-1] + [value] + downward[1:], axis=axis)
    size = value.shape[axis]
    return lax.dynamic_slice_in_dim(
        ordered, (line_count - 1 - line_index) * size, line_count * size, axis
    )


def after(value, *earlier):
    return lax.optimization_barrier((value, *earlier))[0]


def along(sent, pairs, inner_count):
    return lax.ppermute(
        sent,
        "mem",
        [(a * inner_count + b, c * inner_count + b) for a, c in pairs for b in range(inner_count)],
    )


def beside(value, inner_count):
    return along(value, [(0, 1), (1, 0), (2, 3), (3, 2)], inner_count)


def near_half(value, value_beside, line_index):
    return jnp.where(
        line_index % 2 == 1,
        jnp.concatenate([value_beside, value], axis=0),
        jnp.concatenate([value, value_beside], axis=0),
    )


def middle_swap(near, inner_count):
    return along(near, [(1, 2), (2, 1)], inner_count)


def pass_outward(across, inner_count):
    return along(across, [(1, 0), (2, 3)], inner_count)


def attention_kernel(heads, lives_ref, query_ref, key_ref, value_ref, out_ref):
    slots, rows, _ = query_ref.shape
    lanes = 2 * HEAD_DIM
    lane = lax.broadcasted_iota(jnp.int32, (rows, lanes), 1)
    key_at = lax.broadcasted_iota(jnp.int32, (rows, rows), 1)
    first = lane < HEAD_DIM
    for slot in range(slots):
        live = (key_at < lives_ref[0, slot]) | (key_at >= lives_ref[1, slot])
        for pair in range(heads // 2):
            span = slice(pair * lanes, (pair + 1) * lanes)
            query = query_ref[slot, :, span] * HEAD_DIM ** (-0.5)
            key = key_ref[slot, :, span].astype(jnp.bfloat16)
            value = value_ref[slot, :, span].astype(jnp.bfloat16)
            outs = []
            for chosen in (first, ~first):
                scores = lax.dot_general(
                    jnp.where(chosen, query, 0.0).astype(jnp.bfloat16),
                    key,
                    (((1,), (1,)), ((), ())),
                    preferred_element_type=jnp.float32,
                )
                weights = jnp.where(live, jnp.exp(scores), 0.0)
                total = jnp.sum(weights, axis=1, keepdims=True)
                probabilities = (weights / total).astype(jnp.bfloat16)
                outs.append(jnp.dot(probabilities, value, preferred_element_type=jnp.float32))
            out_ref[slot, :, span] = jnp.where(first, outs[0], outs[1])


def columns_kernel(inner_ref, rows_ref, *refs):
    *block_refs, out_ref = refs
    rows = rows_ref[...].astype(jnp.bfloat16)
    parts, _, width = block_refs[0].shape
    for part in range(parts):
        for mask, block_ref in enumerate(block_refs):
            at = (part * len(block_refs) + (inner_ref[0] ^ mask)) * width
            out_ref[:, pl.ds(pl.multiple_of(at, width), width)] = jnp.dot(
                rows, block_ref[part], preferred_element_type=jnp.float32
            )


def times_blocks(rows, inner_index, blocks):
    parts, depth, width = blocks[0].shape
    columns = parts * len(blocks) * width
    return pl.pallas_call(
        columns_kernel,
        out_shape=jax.ShapeDtypeStruct((rows.shape[0], columns), jnp.float32),
        in_specs=[pl.BlockSpec(memory_space=pltpu.SMEM)]
        + [pl.BlockSpec(memory_space=pltpu.VMEM)] * (1 + len(blocks)),
        out_specs=pl.BlockSpec(memory_space=pltpu.VMEM),
        compiler_params=pltpu.CompilerParams(vmem_limit_bytes=24 * 1024 * 1024),
        cost_estimate=pl.CostEstimate(
            flops=2 * rows.shape[0] * depth * columns,
            bytes_accessed=2 * depth * columns + 4 * rows.shape[0] * (depth + columns),
            transcendentals=0,
        ),
    )(inner_index.reshape(1), rows, *blocks)


def attend(lives, queries, keys, values):
    heads = queries.shape[2] // HEAD_DIM
    return pl.pallas_call(
        lambda *refs: attention_kernel(heads, *refs),
        out_shape=jax.ShapeDtypeStruct(queries.shape, jnp.float32),
        in_specs=[pl.BlockSpec(memory_space=pltpu.SMEM)]
        + [pl.BlockSpec(memory_space=pltpu.VMEM)] * 3,
        out_specs=pl.BlockSpec(memory_space=pltpu.VMEM),
        compiler_params=pltpu.CompilerParams(vmem_limit_bytes=24 * 1024 * 1024),
        cost_estimate=pl.CostEstimate(
            flops=4 * queries.shape[0] * queries.shape[1] ** 2 * queries.shape[2],
            bytes_accessed=16 * queries.size,
            transcendentals=queries.shape[0] * queries.shape[1] ** 2 * heads,
        ),
    )(lives, queries, keys, values)


def body(
    question_states,
    passage_cache,
    norm_gain,
    enc_wq,
    enc_wk,
    enc_wv,
    enc_wo,
    dec_wk,
    dec_wv,
    dec_queries,
    passage_ids,
    location,
    question_lengths,
):
    mem_count = lax.axis_size("mem")
    mem_index = lax.axis_index("mem")
    dec_count = lax.axis_size("dec")
    dec_index = lax.axis_index("dec")
    line_count, inner_count = split_mem(mem_count)
    line_index, inner_index = mem_index // inner_count, mem_index % inner_count
    pass_count = passage_ids.shape[1]
    request_total = mem_count * pass_count
    stored_count = passage_cache.shape[0]
    question_rows = question_states.shape[1]
    pair_rows = question_rows + passage_cache.shape[1]
    row_total = CAP * pair_rows
    answer_rows = dec_queries.shape[1]
    local_features = question_states.shape[2]
    heads_width = dec_queries.shape[2]
    heads_here = heads_width // HEAD_DIM
    score_scale = HEAD_DIM ** (-0.5)
    model_width = local_features * dec_count

    cache_row = jnp.take(location, passage_ids.reshape(-1))
    owner_index = cache_row // stored_count
    cache_slot = cache_row % stored_count
    masks = [0]
    for bit in reversed(bits_of(inner_count)):
        masks = masks + [mask + bit for mask in masks]
    owners = mem_index ^ jnp.array(masks)
    served = (owner_index[None, :] == owners[:, None]).astype(jnp.int32)
    served_rank = jnp.cumsum(served, axis=1) - 1
    taken_mask = (served[:, None, :] == 1) & (
        served_rank[:, None, :] == jnp.arange(CAP)[None, :, None]
    )
    request = jnp.sum(jnp.where(taken_mask, jnp.arange(request_total), 0), axis=2)
    plane_asking = request // pass_count
    asking = plane_asking[0]
    filled = jnp.any(taken_mask[0], axis=1)
    local_slot = jnp.sum(jnp.where(taken_mask[0], cache_slot[None, :], 0), axis=1)

    block = model_width // mem_count
    here = line_count // dec_count
    relay = line_count == 4 and inner_count == 4 and dec_count == 2

    def features_for(rows, mask):
        split = rows.reshape(rows.shape[0], -1, inner_count, block)
        picked = lax.dynamic_index_in_dim(split, inner_index ^ mask, 2, keepdims=False)
        return picked.reshape(rows.shape[0], -1)

    query_block = heads_width // inner_count

    def question_part(mask):
        queries_part = lax.dynamic_slice_in_dim(
            dec_queries[0], (inner_index ^ mask) * query_block, query_block, 1
        )
        return jnp.concatenate([features_for(question_states[0], mask), queries_part], axis=1)

    if relay:
        query_beside = beside(enc_wq, inner_count)
    table = jnp.stack(
        [question_part(0)]
        + [swap_mem(question_part(mask), mask, mem_count) for mask in range(1, inner_count)]
    )
    passages = passage_cache[local_slot]
    flat_passages = passages.reshape(-1, local_features)
    plane_passages = [features_for(flat_passages, 0)] + [
        swap_mem(features_for(flat_passages, mask), mask, mem_count) for mask in masks[1:]
    ]
    if relay:
        table = after(table, query_beside)
    came = [
        swap_mem(table, mask, mem_count) for mask in range(inner_count, mem_count, inner_count)
    ]
    if relay:
        enc_wk, enc_wv, *came = lax.optimization_barrier((enc_wk, enc_wv, *came))
        both_beside = beside(jnp.concatenate([enc_wk, enc_wv], axis=0), inner_count)
        query_near = near_half(after(enc_wq, *came), query_beside, line_index)
        across_query = middle_swap(query_near, inner_count)
    table = jnp.concatenate([table] + came, axis=0)
    plane_parts = table[plane_asking ^ mem_index]
    plane_questions = plane_parts[..., : here * block]
    plane_raw = jnp.concatenate(
        [
            plane_questions,
            jnp.stack(plane_passages).reshape(len(masks), CAP, -1, here * block),
        ],
        axis=2,
    ).reshape(-1, here * block)
    line_gain = lax.dynamic_index_in_dim(
        lax.dynamic_slice_in_dim(
            norm_gain.reshape(line_count, inner_count, block), dec_index * here, here, 0
        ),
        inner_index,
        1,
        keepdims=False,
    ).reshape(-1)
    plane_rows = (plane_raw.astype(jnp.float32) * line_gain).astype(jnp.bfloat16)

    place = {mask: at for at, mask in enumerate(masks)}
    own_parts = jnp.stack(
        [plane_parts[0]]
        + [
            swap_mem(plane_parts[place[mask]], mask, mem_count)
            for mask in range(1, inner_count)
        ]
    )[jnp.arange(inner_count) ^ inner_index]
    own_features = own_parts[..., : here * block].reshape(
        inner_count, CAP, question_rows, here, block
    )
    asked_states = jnp.transpose(own_features, (1, 2, 3, 0, 4)).reshape(CAP, question_rows, -1)
    asked_queries = jnp.transpose(own_parts[..., here * block :], (1, 2, 0, 3)).reshape(
        CAP, answer_rows, -1
    )
    asked_queries = over_dec(asked_queries, dec_index, dec_count)
    local_rows = jnp.concatenate([asked_states, passages], axis=1).reshape(row_total, -1)
    wide_rows = local_rows.astype(jnp.float32)
    squares = jnp.sum(jnp.square(wide_rows), axis=1, keepdims=True)
    row_scale = lax.rsqrt(dec_sum(squares, dec_count) / model_width + NORM_EPSILON)

    upper = line_index >= line_count // 2
    middle = (line_index == 1) | (line_index == 2)
    weights = (enc_wq, enc_wk, enc_wv)
    near_rows, far_rows = over_dec_halves(plane_rows, upper, dec_index, dec_count)
    if relay:
        block_rows = enc_wk.shape[0]
        nears = [
            query_near,
            near_half(enc_wk, both_beside[:block_rows], line_index),
            near_half(enc_wv, both_beside[block_rows:], line_index),
        ]
        near_rows, far_rows, both_beside, across_query = lax.optimization_barrier(
            (near_rows, far_rows, both_beside, across_query)
        )
        out_beside = beside(after(enc_wo, both_beside), inner_count)
        outward_query = pass_outward(across_query, inner_count)
        across_key = middle_swap(after(nears[1], across_query), inner_count)
        outward_key = pass_outward(across_key, inner_count)
        across_value = middle_swap(after(nears[2], across_key), inner_count)
        outward_value = pass_outward(after(across_value, outward_key), inner_count)
        out_near = jnp.stack([enc_wo, out_beside])
        out_near = jnp.where(line_index % 2 == 1, out_near[::-1], out_near)
        out_far = []
        earlier = (across_value, outward_value)
        for part in range(2):
            across = middle_swap(after(out_near[part], earlier[0]), inner_count)
            outward = pass_outward(after(across, earlier[1]), inner_count)
            earlier = (across, outward)
            out_far.append(jnp.where(middle, across, outward)[None])
        out_pieces = []
        for piece in [out_near] + out_far:
            from_chip = swap_mem(piece, 2, mem_count)
            out_pieces.append(
                (
                    piece,
                    swap_mem(piece, 1, mem_count),
                    from_chip,
                    swap_mem(from_chip, 1, mem_count),
                )
            )
        fars = [
            jnp.where(middle, across, outward)
            for across, outward in (
                (across_query, outward_query),
                (across_key, outward_key),
                (across_value, outward_value),
            )
        ]
    else:
        nears, fars = [], []
        for weight in weights:
            whole = gather_line(weight, 0, line_index, line_count, inner_count)
            half = whole.shape[0] // 2
            nears.append(jnp.where(upper, whole[half:], whole[:half]))
            fars.append(jnp.where(upper, whole[:half], whole[half:]))

    def project(near_weight, far_weight, *earlier):
        def rows_sum(low, high):
            return jnp.dot(
                near_rows[low:high], near_weight, preferred_element_type=jnp.float32
            ) + jnp.dot(far_rows[low:high], far_weight, preferred_element_type=jnp.float32)

        rows = near_rows.shape[0]
        total = None
        for bit in bits_of(inner_count):
            rows //= 2
            if total is None:
                given, kept = rows_sum(rows, 2 * rows), rows_sum(0, rows)
                if earlier:
                    given = after(given, *earlier)
            else:
                given, kept = total[rows:], total[:rows]
            total = kept + swap_mem(given.astype(jnp.bfloat16), bit, mem_count).astype(
                jnp.float32
            )
        return (total * row_scale).reshape(CAP, pair_rows, -1)

    ties = ((across_key, out_beside), (across_value,), (out_pieces[0][2],)) if relay else ((),) * 3
    queries, enc_keys, enc_values = (
        project(near, far, *tie) for near, far, tie in zip(nears, fars, ties)
    )
    lengths_here = question_lengths[asking]
    positions = jnp.arange(pair_rows)
    live_keys = (
        (positions[None, :] >= question_rows) | (positions[None, :] < lengths_here[:, None])
    ).astype(jnp.float32)
    lives = jnp.stack([lengths_here, jnp.full_like(lengths_here, question_rows)])
    context = attend(lives, queries, enc_keys, enc_values).reshape(row_total, heads_width)
    if relay:
        near_sum, *far_sums = (times_blocks(context, inner_index, blocks) for blocks in out_pieces)
        own_near = upper == (dec_index == 1)

        def to_owner(value, near):
            pairs = []
            for at in range(mem_count):
                half = at // (mem_count // 2)
                goal = half if near else 1 - half
                pairs.append((at * 2 + 1 - goal, at * 2 + goal))
            return lax.ppermute(value.astype(jnp.bfloat16), ("mem", "dec"), pairs)

        near_came = to_owner(near_sum, True)
        far_came = [to_owner(value, False) for value in far_sums]
        attended = jnp.where(
            own_near,
            near_sum + near_came.astype(jnp.float32),
            jnp.concatenate(
                [a + b.astype(jnp.float32) for a, b in zip(far_sums, far_came)], axis=1
            ),
        )
    else:
        out_weight = lax.all_gather(enc_wo, "mem", axis=1, tiled=True)
        partial_out = jnp.dot(
            context.astype(jnp.bfloat16), out_weight, preferred_element_type=jnp.float32
        )
        attended = lax.psum_scatter(
            partial_out.astype(jnp.bfloat16), "dec", scatter_dimension=1, tiled=True
        ).astype(jnp.float32)
    encoded = (wide_rows + attended).astype(jnp.bfloat16)

    head_total = asked_queries.shape[2] // HEAD_DIM
    own_head = (
        jnp.arange(head_total * HEAD_DIM)[None, :] // HEAD_DIM == jnp.arange(head_total)[:, None]
    )
    spread = jnp.where(own_head[None, :, None, :], asked_queries[:, None], 0)
    wide_queries = lax.dot_general(
        spread.reshape(-1, head_total * HEAD_DIM),
        dec_wk,
        (((1,), (1,)), ((), ())),
        preferred_element_type=jnp.float32,
    ).astype(jnp.bfloat16)
    slot_rows = encoded.reshape(CAP, pair_rows, local_features)
    cross_scores = dec_sum(
        jnp.einsum(
            "cmf,cjf->cmj",
            wide_queries.reshape(CAP, head_total * answer_rows, local_features),
            slot_rows,
            preferred_element_type=jnp.float32,
        ),
        dec_count,
    )
    keep_keys = live_keys * filled.astype(jnp.float32)[:, None]
    cross_weight = jnp.exp(cross_scores * score_scale) * keep_keys[:, None, :]
    dec_values = jnp.dot(encoded, dec_wv, preferred_element_type=jnp.float32).astype(jnp.bfloat16)
    products = jnp.einsum(
        "cmj,cjv->cmv",
        cross_weight.astype(jnp.bfloat16),
        dec_values.reshape(CAP, pair_rows, -1),
        preferred_element_type=jnp.float32,
    ).reshape(CAP, head_total, answer_rows, -1)
    sums = jnp.sum(jnp.where(own_head[None, :, None, :], products, 0.0), axis=1)
    blocks = sums.reshape(CAP, answer_rows, dec_count, heads_width)

    def block_of(index):
        return lax.dynamic_index_in_dim(blocks, index, 2, keepdims=False)

    numerators = block_of(dec_index)
    for step in range(1, dec_count):
        numerators = numerators + lax.ppermute(
            block_of((dec_index + step) % dec_count).astype(jnp.bfloat16),
            "dec",
            [(i, (i + step) % dec_count) for i in range(dec_count)],
        ).astype(jnp.float32)
    every_denominator = jnp.sum(cross_weight, axis=2).reshape(CAP, head_total, answer_rows)
    denominators = lax.dynamic_slice_in_dim(
        every_denominator, dec_index * heads_here, heads_here, 1
    )
    both = jnp.concatenate(
        [
            numerators.reshape(CAP, -1),
            jnp.transpose(denominators, (0, 2, 1)).reshape(CAP, -1),
        ],
        axis=1,
    )
    targets = (
        (asking[:, None] == jnp.arange(mem_count)[None, :]) & filled[:, None]
    ).astype(jnp.float32)
    back = sum(targets[c][:, None] * both[c][None, :] for c in range(CAP))
    got = lax.all_to_all(
        back.astype(jnp.bfloat16), "mem", split_axis=0, concat_axis=0, tiled=True
    ).astype(jnp.float32)
    got_sum = jnp.sum(got, axis=0)
    numerator_sum = got_sum[: answer_rows * heads_width]
    denominator_sum = got_sum[answer_rows * heads_width :]
    answer = (
        numerator_sum.reshape(answer_rows, heads_here, HEAD_DIM)
        / denominator_sum.reshape(answer_rows, heads_here)[:, :, None]
    )
    return answer.reshape(1, answer_rows, heads_width).astype(jnp.bfloat16)


def solution(mesh):
    in_specs = (
        P("mem", None, "dec"),
        P("mem", None, "dec"),
        P(),
        P("mem", "dec"),
        P("mem", "dec"),
        P("mem", "dec"),
        P("dec", "mem"),
        P("dec", None),
        P("dec", None),
        P("mem", None, "dec"),
        P(),
        P(),
        P(),
    )
    out_specs = P("mem", None, "dec")
    return jax.shard_map(body, mesh=mesh, in_specs=in_specs, out_specs=out_specs, check_vma=False)
```
